32 devices in a mesh: seq: 8 (over z, y), grp: 4 (over x, core).
Axes of the slice: x: 2, y: 2, z: 4, core: 2. Of those that a mesh axis runs over, the one named last changes fastest.
Arguments:
- queries: bfloat16 [8, 4096], P('seq'), may hold values from -6 to 6
- prompt_keys: bfloat16 [32768, 512], P(('seq', 'grp')), may hold values from -15 to 15
- prompt_values: bfloat16 [32768, 512], P(('seq', 'grp')), may hold values from -6 to 6
- suffix_keys: bfloat16 [8, 1024, 512], P('seq', 'grp'), may hold values from -16 to 16
- suffix_values: bfloat16 [8, 1024, 512], P('seq', 'grp'), may hold values from -6 to 6
- lengths: int32 [8], P('seq'), may hold values from 1 to 1024, as said below
Outputs:
- attended: bfloat16 [8, 4096], P('seq', 'grp')
The draws below stay inside these ranges and needn't reach their ends.
Inputs may be any that keep to these rules, and one draw needn't show every extreme that they name: `lengths`: some response has exactly 1024 live positions.
All inputs are finite; a program needn't handle non-finite values.
Results may differ from the reference program's by a relative error of at most 0.003.
Values may be sent and summed in bfloat16 or wider, within the bound.
No kernel may reach another device: no remote copies, remote signals or barrier semaphores. Data moves between devices by JAX's collectives and lax.ppermute only.
A program may use at most 64 MiB of HBM per device.

```python
import math
import jax
import jax.numpy as jnp
from jax import lax

Q_HEADS = 32
KV_HEADS = 4
HEAD_DIM = 128
GROUP = 8
PRE_DEV = 1024
SUF_DEV = 256
RESPONSES = 8
PROMPT = 32768
SUFFIX = 1024


def draw_queries(key, part):
    key = jax.random.fold_in(key, 1)
    base = jnp.clip(jax.random.normal(key, (RESPONSES, Q_HEADS, HEAD_DIM), jnp.float32), -6.0, 6.0)
    return base.reshape(RESPONSES, Q_HEADS * HEAD_DIM).astype(jnp.bfloat16)


def draw_prompt_keys(key, part):
    key = jax.random.fold_in(key, 2)
    base = jnp.clip(2.5 * jax.random.normal(key, (PROMPT, KV_HEADS, HEAD_DIM), jnp.float32), -15.0, 15.0)
    return base.reshape(PROMPT, KV_HEADS * HEAD_DIM).astype(jnp.bfloat16)


def draw_lengths(key, part):
    key = jax.random.fold_in(key, 3)
    drawn = jax.random.randint(key, (RESPONSES,), 1, SUFFIX + 1, dtype=jnp.int32)
    which = jax.random.randint(jax.random.fold_in(key, 4), (), 0, RESPONSES, dtype=jnp.int32)
    return drawn.at[which].set(SUFFIX)


def level_of(rng, shape, cuts, low, high):
    def one(dim, parts):
        draws = jax.random.uniform(jax.random.fold_in(jax.random.fold_in(rng, 6), dim), (parts,), jnp.float32, low / len(cuts), high / len(cuts))
        return jnp.repeat(jnp.exp(draws), shape[dim] // parts).reshape((-1,) + (1,) * (len(shape) - dim - 1))

    factor_of = one(*cuts[0])
    for cut in cuts[1:]:
        factor_of = factor_of * one(*cut)
    return factor_of


def scatter_about(stream_key, shape, width, limit, pieces=(), kind=jnp.bfloat16):
    gain = level_of(stream_key, shape, pieces, -0.22, 0.18) if pieces else 1.0
    values = jax.random.normal(stream_key, shape, jnp.float32) * width * gain
    return jnp.minimum(jnp.maximum(values, -limit), limit).astype(kind)


def setup_inputs(seed: int = 0) -> dict:
    key_list = jax.random.split(jax.random.key(seed), 7)
    queries = draw_queries(jax.random.fold_in(key_list[6], 71), 0)
    prompt_keys = draw_prompt_keys(jax.random.fold_in(key_list[6], 71), 0)
    prompt_values = scatter_about(key_list[2], (PROMPT, KV_HEADS * HEAD_DIM), 1.0, 6.0, ((0, 32),))
    suffix_keys = scatter_about(key_list[3], (RESPONSES, SUFFIX, KV_HEADS * HEAD_DIM), 4.0, 16.0, ((0, 8), (1, 4)))
    suffix_values = scatter_about(key_list[4], (RESPONSES, SUFFIX, KV_HEADS * HEAD_DIM), 1.0, 6.0, ((0, 8), (1, 4)))
    lengths = draw_lengths(jax.random.fold_in(key_list[6], 71), 0)
    return dict(queries=queries, prompt_keys=prompt_keys, prompt_values=prompt_values, suffix_keys=suffix_keys, suffix_values=suffix_values, lengths=lengths)


def fold_in_block(carry, peak, total, output):
    top, acc_total, acc_output = carry
    new_top = jnp.maximum(top, peak)
    old_factor = jnp.exp(top - new_top)
    new_factor = jnp.exp(peak - new_top)
    acc_total = acc_total * old_factor + total * new_factor
    acc_output = acc_output * old_factor[..., None] + output * new_factor[..., None]
    return (new_top, acc_total, acc_output)

def reference(queries, prompt_keys, prompt_values, suffix_keys, suffix_values, lengths):
    scale = 1.0 / math.sqrt(HEAD_DIM)
    query_all = queries.astype(jnp.float32).reshape(RESPONSES, KV_HEADS, GROUP, HEAD_DIM)
    key_blocks = prompt_keys.reshape(PROMPT // PRE_DEV, PRE_DEV, KV_HEADS, HEAD_DIM)
    value_blocks = prompt_values.reshape(PROMPT // PRE_DEV, PRE_DEV, KV_HEADS, HEAD_DIM)
    start = (jnp.full((RESPONSES, KV_HEADS, GROUP), -1e+30, jnp.float32), jnp.zeros((RESPONSES, KV_HEADS, GROUP), jnp.float32), jnp.zeros((RESPONSES, KV_HEADS, GROUP, HEAD_DIM), jnp.float32))

    def prompt_step(carry, blocks):
        key_block, value_block = blocks
        scores = jnp.einsum('rjgd,tjd->rjgt', query_all, key_block.astype(jnp.float32), precision=lax.Precision.HIGHEST) * scale
        peak = lax.optimization_barrier(jnp.max(scores, axis=-1))
        expo = jnp.exp(scores - peak[..., None])
        total = lax.optimization_barrier(jnp.sum(expo, axis=-1))
        weights = expo.astype(jnp.bfloat16).astype(jnp.float32)
        output = jnp.einsum('rjgt,tjd->rjgd', weights, value_block.astype(jnp.float32), precision=lax.Precision.HIGHEST)
        return (fold_in_block(carry, peak, total, output), None)
    carry, _ = lax.scan(prompt_step, start, (key_blocks, value_blocks))
    suffix_k = suffix_keys.reshape(RESPONSES, SUFFIX // SUF_DEV, SUF_DEV, KV_HEADS, HEAD_DIM)
    suffix_v = suffix_values.reshape(RESPONSES, SUFFIX // SUF_DEV, SUF_DEV, KV_HEADS, HEAD_DIM)
    for block in range(SUFFIX // SUF_DEV):
        scores = jnp.einsum('rjgd,rtjd->rjgt', query_all, suffix_k[:, block].astype(jnp.float32), precision=lax.Precision.HIGHEST) * scale
        position = block * SUF_DEV + jnp.arange(SUF_DEV, dtype=jnp.int32)
        live = (position[None, :] < lengths[:, None])[:, None, None, :]
        masked = jnp.where(live, scores, -1e+30)
        peak = lax.optimization_barrier(jnp.max(masked, axis=-1))
        expo = jnp.where(live, jnp.exp(masked - peak[..., None]), 0.0)
        total = lax.optimization_barrier(jnp.sum(expo, axis=-1))
        weights = expo.astype(jnp.bfloat16).astype(jnp.float32)
        output = jnp.einsum('rjgt,rtjd->rjgd', weights, suffix_v[:, block].astype(jnp.float32), precision=lax.Precision.HIGHEST)
        carry = fold_in_block(carry, peak, total, output)
    top, total, output = carry
    result = output / total[..., None]
    return result.reshape(RESPONSES, Q_HEADS * HEAD_DIM).astype(jnp.bfloat16)
```

```python
import functools
import math

import jax
import jax.numpy as jnp
from jax import lax
from jax.experimental import pallas as pl
from jax.experimental.pallas import tpu as pltpu
from jax.sharding import PartitionSpec as P

Q_HEADS = 32
KV_HEADS = 4
HEAD_DIM = 128
GROUP = 8
BLOCK = 8
ROWS = GROUP + 1
WIDTH = ROWS * HEAD_DIM
LOG2_SCALE = math.log2(math.e) / math.sqrt(HEAD_DIM)
LOWEST = -1e30

VMEM = pl.BlockSpec(memory_space=pltpu.VMEM)
SMEM = pl.BlockSpec(memory_space=pltpu.SMEM)


def in_vmem(x):
    return pltpu.with_memory_space_constraint(x, pltpu.VMEM)


def spread_kernel(query_ref, out_ref):
    query = query_ref[...].astype(jnp.float32)
    rows = [query[:, h * HEAD_DIM : (h + 1) * HEAD_DIM] for h in range(Q_HEADS)]
    rows = jnp.concatenate(rows, axis=0).astype(out_ref.dtype)
    out_ref[...] = jnp.broadcast_to(rows[None], out_ref.shape)


def dot_rows(a, b):
    return lax.dot_general(a, b, (((1,), (1,)), ((), ())), preferred_element_type=jnp.float32)


def partial_kernel(lengths_ref, query_ref, key_ref, value_ref, own_key_ref, own_value_ref, out_ref):
    count = query_ref.shape[0]
    span = own_key_ref.shape[0]
    me = lax.axis_index("seq")
    position = lax.axis_index("grp") * span + lax.broadcasted_iota(jnp.int32, (GROUP, span), 1)
    live = position < lengths_ref[0]
    own_query = query_ref[me].astype(jnp.float32)
    chunks = out_ref.reshape(out_ref.shape[0] * ROWS, HEAD_DIM)

    own = []
    for j in range(KV_HEADS):
        columns = slice(j * HEAD_DIM, (j + 1) * HEAD_DIM)
        query = own_query[j * GROUP : (j + 1) * GROUP].astype(jnp.bfloat16)
        scores = jnp.where(live, dot_rows(query, own_key_ref[:, columns]), LOWEST)
        peak = jnp.max(scores, axis=1, keepdims=True)
        expo = jnp.where(live, jnp.exp2((scores - peak) * LOG2_SCALE), 0.0)
        total = jnp.sum(expo, axis=1, keepdims=True)
        output = jnp.dot(
            expo.astype(jnp.bfloat16), own_value_ref[:, columns], preferred_element_type=jnp.float32
        )
        own.append((peak, total, output))

    def one_block(block):
        queries = query_ref[pl.ds(block * BLOCK, BLOCK)].astype(jnp.float32)
        response = block * BLOCK + lax.broadcasted_iota(jnp.int32, (BLOCK, GROUP, 1), 0)
        mine = response == me
        lane = lax.broadcasted_iota(jnp.int32, (BLOCK * GROUP, HEAD_DIM), 1)
        peaks = jnp.zeros((BLOCK * GROUP, HEAD_DIM), jnp.float32)
        totals = jnp.zeros((BLOCK * GROUP, HEAD_DIM), jnp.float32)
        for j in range(KV_HEADS):
            columns = slice(j * HEAD_DIM, (j + 1) * HEAD_DIM)
            query = queries[:, j * GROUP : (j + 1) * GROUP].reshape(BLOCK * GROUP, HEAD_DIM)
            scores = dot_rows(query.astype(jnp.bfloat16), key_ref[:, columns])
            peak = jnp.max(scores, axis=1, keepdims=True)
            expo = jnp.exp2((scores - peak) * LOG2_SCALE)
            total = jnp.sum(expo, axis=1, keepdims=True)
            output = jnp.dot(
                expo.astype(jnp.bfloat16), value_ref[:, columns], preferred_element_type=jnp.float32
            )
            own_peak, own_total, own_output = own[j]
            peak = peak.reshape(BLOCK, GROUP, 1)
            total = total.reshape(BLOCK, GROUP, 1)
            output = output.reshape(BLOCK, GROUP, HEAD_DIM)
            joined = jnp.where(mine, jnp.maximum(peak, own_peak[None]), peak)
            factor = jnp.exp2((peak - joined) * LOG2_SCALE)
            own_factor = jnp.where(mine, jnp.exp2((own_peak[None] - joined) * LOG2_SCALE), 0.0)
            total = total * factor + own_total[None] * own_factor
            output = output * factor + own_output[None] * own_factor
            peaks = jnp.where(lane == j, joined.reshape(BLOCK * GROUP, 1), peaks)
            totals = jnp.where(lane == j, total.reshape(BLOCK * GROUP, 1), totals)
            for r in range(BLOCK):
                chunk = ((block * BLOCK + r) * KV_HEADS + j) * ROWS
                chunks[pl.ds(chunk, GROUP), :] = output[r]
        sums = jnp.concatenate([peaks, totals], axis=0).T
        for r in range(BLOCK):
            for j in range(KV_HEADS):
                chunk = ((block * BLOCK + r) * KV_HEADS + j) * ROWS
                chunks[pl.ds(chunk + GROUP, 1), :] = sums[j : j + 1]

    if count == BLOCK:
        one_block(0)
    else:
        pl.loop(0, count // BLOCK)(one_block)


def join_kernel(parts_ref, out_ref):
    parts = parts_ref.shape[0]
    chunks = parts_ref.reshape(parts * ROWS, HEAD_DIM)
    sums = parts_ref[:, 0, GROUP * HEAD_DIM :]
    offset = (lax.axis_index("seq") % BLOCK) * GROUP
    sums = pltpu.roll(sums, (HEAD_DIM - offset) % HEAD_DIM, 1).T
    peaks = sums[:GROUP]
    totals = sums[BLOCK * GROUP : BLOCK * GROUP + GROUP]
    factor = jnp.exp2((peaks - jnp.max(peaks, axis=1, keepdims=True)) * LOG2_SCALE)
    total = jnp.sum(factor * totals, axis=1, keepdims=True)
    acc = [jnp.zeros((GROUP, HEAD_DIM), jnp.float32)] * 4
    for i in range(parts):
        acc[i % 4] += factor[:, i : i + 1] * chunks[i * ROWS : i * ROWS + GROUP, :]
    output = ((acc[0] + acc[1]) + (acc[2] + acc[3])) / total
    for h in range(GROUP):
        out_ref[:, h * HEAD_DIM : (h + 1) * HEAD_DIM] = output[h : h + 1].astype(out_ref.dtype)


def on_device(seq, grp, queries, prompt_keys, prompt_values, suffix_keys, suffix_values, lengths):
    copies = pl.pallas_call(
        spread_kernel,
        out_shape=pltpu.VMEM((seq, Q_HEADS, HEAD_DIM), queries.dtype),
        in_specs=[VMEM],
        out_specs=VMEM,
    )(queries)
    every = lax.all_to_all(copies, "seq", 0, 0, tiled=True)
    span = suffix_keys.shape[1]
    width = KV_HEADS * HEAD_DIM
    partial = pl.pallas_call(
        partial_kernel,
        out_shape=pltpu.VMEM((seq * grp, 1, WIDTH), jnp.float32),
        in_specs=[SMEM] + [VMEM] * 5,
        out_specs=VMEM,
    )(
        lengths,
        in_vmem(every),
        in_vmem(prompt_keys),
        in_vmem(prompt_values),
        in_vmem(suffix_keys.reshape(span, width)),
        in_vmem(suffix_values.reshape(span, width)),
    )
    parts = lax.all_to_all(partial, ("seq", "grp"), 0, 0, tiled=True)
    return pl.pallas_call(
        join_kernel,
        out_shape=jax.ShapeDtypeStruct((1, GROUP * HEAD_DIM), queries.dtype),
        in_specs=[VMEM],
        out_specs=VMEM,
    )(in_vmem(parts))


def solution(mesh):
    in_specs = (
        P("seq", None),
        P(("seq", "grp"), None),
        P(("seq", "grp"), None),
        P("seq", "grp", None),
        P("seq", "grp", None),
        P("seq"),
    )
    return jax.shard_map(
        functools.partial(on_device, mesh.shape["seq"], mesh.shape["grp"]),
        mesh=mesh,
        in_specs=in_specs,
        out_specs=P("seq", "grp"),
        check_vma=False,
    )
```

```python
import functools
import math

import jax
import jax.numpy as jnp
from jax import lax
from jax.experimental import pallas as pl
from jax.experimental.pallas import tpu as pltpu
from jax.sharding import PartitionSpec as P

Q_HEADS = 32
KV_HEADS = 4
HEAD_DIM = 128
GROUP = 8
BLOCK = 8
ROWS = GROUP + 1
WIDTH = ROWS * HEAD_DIM
LOG2_SCALE = math.log2(math.e) / math.sqrt(HEAD_DIM)
LOWEST = -1e30

VMEM = pl.BlockSpec(memory_space=pltpu.VMEM)
SMEM = pl.BlockSpec(memory_space=pltpu.SMEM)


def in_vmem(x):
    return pltpu.with_memory_space_constraint(x, pltpu.VMEM)


def spread_kernel(query_ref, out_ref):
    query = query_ref[...].astype(jnp.float32)
    rows = [query[:, h * HEAD_DIM : (h + 1) * HEAD_DIM] for h in range(Q_HEADS)]
    rows = jnp.concatenate(rows, axis=0).astype(out_ref.dtype)
    out_ref[...] = jnp.broadcast_to(rows[None], out_ref.shape)


def dot_rows(a, b):
    return lax.dot_general(a, b, (((1,), (1,)), ((), ())), preferred_element_type=jnp.float32)


def own_kernel(lengths_ref, query_ref, own_key_ref, own_value_ref, key_ref, value_ref, own_ref, key_out, value_out, sems):
    copies = [
        pltpu.make_async_copy(key_ref, key_out, sems.at[0]),
        pltpu.make_async_copy(value_ref, value_out, sems.at[1]),
    ]
    for copy in copies:
        copy.start()
    span = own_key_ref.shape[0]
    position = lax.axis_index("grp") * span + lax.broadcasted_iota(jnp.int32, (GROUP, span), 1)
    live = position < lengths_ref[0]
    query = query_ref[0].astype(jnp.float32)
    for j in range(KV_HEADS):
        columns = slice(j * HEAD_DIM, (j + 1) * HEAD_DIM)
        part = query[j * GROUP : (j + 1) * GROUP].astype(jnp.bfloat16)
        scores = jnp.where(live, dot_rows(part, own_key_ref[:, columns]), LOWEST)
        peak = jnp.max(scores, axis=1, keepdims=True)
        expo = jnp.where(live, jnp.exp2((scores - peak) * LOG2_SCALE), 0.0)
        total = jnp.sum(expo, axis=1, keepdims=True)
        output = jnp.dot(
            expo.astype(jnp.bfloat16), own_value_ref[:, columns], preferred_element_type=jnp.float32
        )
        own_ref[j, 0] = output
        own_ref[j, 1] = jnp.broadcast_to(peak, (GROUP, HEAD_DIM))
        own_ref[j, 2] = jnp.broadcast_to(total, (GROUP, HEAD_DIM))
    for copy in copies:
        copy.wait()


def partial_kernel(query_ref, key_ref, value_ref, own_ref, out_ref):
    count = query_ref.shape[0]
    me = lax.axis_index("seq")
    chunks = out_ref.reshape(out_ref.shape[0] * ROWS, HEAD_DIM)

    def one_block(block):
        queries = query_ref[pl.ds(block * BLOCK, BLOCK)].astype(jnp.float32)
        response = block * BLOCK + lax.broadcasted_iota(jnp.int32, (BLOCK, GROUP, 1), 0)
        mine = response == me
        lane = lax.broadcasted_iota(jnp.int32, (BLOCK * GROUP, HEAD_DIM), 1)
        peaks = jnp.zeros((BLOCK * GROUP, HEAD_DIM), jnp.float32)
        totals = jnp.zeros((BLOCK * GROUP, HEAD_DIM), jnp.float32)
        for j in range(KV_HEADS):
            columns = slice(j * HEAD_DIM, (j + 1) * HEAD_DIM)
            query = queries[:, j * GROUP : (j + 1) * GROUP].reshape(BLOCK * GROUP, HEAD_DIM)
            scores = dot_rows(query.astype(jnp.bfloat16), key_ref[:, columns])
            peak = jnp.max(scores, axis=1, keepdims=True)
            expo = jnp.exp2((scores - peak) * LOG2_SCALE)
            total = jnp.sum(expo, axis=1, keepdims=True)
            output = jnp.dot(
                expo.astype(jnp.bfloat16), value_ref[:, columns], preferred_element_type=jnp.float32
            )
            own_output, own_peak, own_total = own_ref[j, 0], own_ref[j, 1, :, :1], own_ref[j, 2, :, :1]
            peak = peak.reshape(BLOCK, GROUP, 1)
            total = total.reshape(BLOCK, GROUP, 1)
            output = output.reshape(BLOCK, GROUP, HEAD_DIM)
            joined = jnp.where(mine, jnp.maximum(peak, own_peak[None]), peak)
            factor = jnp.exp2((peak - joined) * LOG2_SCALE)
            own_factor = jnp.where(mine, jnp.exp2((own_peak[None] - joined) * LOG2_SCALE), 0.0)
            total = total * factor + own_total[None] * own_factor
            output = output * factor + own_output[None] * own_factor
            peaks = jnp.where(lane == j, joined.reshape(BLOCK * GROUP, 1), peaks)
            totals = jnp.where(lane == j, total.reshape(BLOCK * GROUP, 1), totals)
            for r in range(BLOCK):
                chunk = ((block * BLOCK + r) * KV_HEADS + j) * ROWS
                chunks[pl.ds(chunk, GROUP), :] = output[r]
        sums = jnp.concatenate([peaks, totals], axis=0).T
        for r in range(BLOCK):
            for j in range(KV_HEADS):
                chunk = ((block * BLOCK + r) * KV_HEADS + j) * ROWS
                chunks[pl.ds(chunk + GROUP, 1), :] = sums[j : j + 1]

    if count == BLOCK:
        one_block(0)
    else:
        pl.loop(0, count // BLOCK)(one_block)


def join_kernel(parts_ref, out_ref):
    parts = parts_ref.shape[0]
    chunks = parts_ref.reshape(parts * ROWS, HEAD_DIM)
    sums = parts_ref[:, 0, GROUP * HEAD_DIM :]
    offset = (lax.axis_index("seq") % BLOCK) * GROUP
    sums = pltpu.roll(sums, (HEAD_DIM - offset) % HEAD_DIM, 1).T
    peaks = sums[:GROUP]
    totals = sums[BLOCK * GROUP : BLOCK * GROUP + GROUP]
    factor = jnp.exp2((peaks - jnp.max(peaks, axis=1, keepdims=True)) * LOG2_SCALE)
    total = jnp.sum(factor * totals, axis=1, keepdims=True)
    acc = [jnp.zeros((GROUP, HEAD_DIM), jnp.float32)] * 4
    for i in range(parts):
        acc[i % 4] += factor[:, i : i + 1] * chunks[i * ROWS : i * ROWS + GROUP, :]
    output = ((acc[0] + acc[1]) + (acc[2] + acc[3])) / total
    for h in range(GROUP):
        out_ref[:, h * HEAD_DIM : (h + 1) * HEAD_DIM] = output[h : h + 1].astype(out_ref.dtype)


def on_device(seq, grp, queries, prompt_keys, prompt_values, suffix_keys, suffix_values, lengths):
    copies = pl.pallas_call(
        spread_kernel,
        out_shape=pltpu.VMEM((seq, Q_HEADS, HEAD_DIM), queries.dtype),
        in_specs=[VMEM],
        out_specs=VMEM,
    )(queries)
    every = lax.all_to_all(copies, "seq", 0, 0, tiled=True)
    span = suffix_keys.shape[1]
    width = KV_HEADS * HEAD_DIM
    own, keys, values = pl.pallas_call(
        own_kernel,
        out_shape=(
            pltpu.VMEM((KV_HEADS, 3, GROUP, HEAD_DIM), jnp.float32),
            pltpu.VMEM(prompt_keys.shape, prompt_keys.dtype),
            pltpu.VMEM(prompt_values.shape, prompt_values.dtype),
        ),
        in_specs=[SMEM] + [VMEM] * 3 + [pl.BlockSpec(memory_space=pl.ANY)] * 2,
        out_specs=(VMEM, VMEM, VMEM),
        scratch_shapes=[pltpu.SemaphoreType.DMA((2,))],
    )(
        lengths,
        in_vmem(copies),
        suffix_keys.reshape(span, width),
        suffix_values.reshape(span, width),
        prompt_keys,
        prompt_values,
    )
    partial = pl.pallas_call(
        partial_kernel,
        out_shape=pltpu.VMEM((seq * grp, 1, WIDTH), jnp.float32),
        in_specs=[VMEM] * 4,
        out_specs=VMEM,
    )(in_vmem(every), in_vmem(keys), in_vmem(values), in_vmem(own))
    parts = lax.all_to_all(partial, ("seq", "grp"), 0, 0, tiled=True)
    return pl.pallas_call(
        join_kernel,
        out_shape=jax.ShapeDtypeStruct((1, GROUP * HEAD_DIM), queries.dtype),
        in_specs=[VMEM],
        out_specs=VMEM,
    )(in_vmem(parts))


def solution(mesh):
    in_specs = (
        P("seq", None),
        P(("seq", "grp"), None),
        P(("seq", "grp"), None),
        P("seq", "grp", None),
        P("seq", "grp", None),
        P("seq"),
    )
    return jax.shard_map(
        functools.partial(on_device, mesh.shape["seq"], mesh.shape["grp"]),
        mesh=mesh,
        in_specs=in_specs,
        out_specs=P("seq", "grp"),
        check_vma=False,
    )
```

```python
import functools
import math

import jax
import jax.numpy as jnp
from jax import lax
from jax.experimental import pallas as pl
from jax.experimental.pallas import tpu as pltpu
from jax.sharding import PartitionSpec as P

Q_HEADS = 32
KV_HEADS = 4
HEAD_DIM = 128
GROUP = 8
PAIRS = KV_HEADS // 2
PAIR_DIM = 2 * HEAD_DIM
BLOCK = 8
BLOCK_ROWS = BLOCK * GROUP
ROWS = GROUP + 1
WIDTH = ROWS * HEAD_DIM
SCALE = 1.0 / math.sqrt(HEAD_DIM)
LOWEST = -1e30

VMEM = pl.BlockSpec(memory_space=pltpu.VMEM)
ANY = pl.BlockSpec(memory_space=pl.ANY)


def in_vmem(x):
    return pltpu.with_memory_space_constraint(x, pltpu.VMEM)


def spread_kernel(query_ref, key_ref, out_ref, key_out, query, copies, sems):
    query_in = pltpu.make_async_copy(query_ref, query, sems.at[0])
    keys_in = pltpu.make_async_copy(key_ref, key_out, sems.at[1])
    copies_out = pltpu.make_async_copy(copies, out_ref, sems.at[2])
    query_in.start()
    keys_in.start()
    query_in.wait()
    row = query[...].astype(jnp.float32)
    rows = [row[:, h * HEAD_DIM : (h + 1) * HEAD_DIM] for h in range(Q_HEADS)]
    rows = jnp.concatenate(rows, axis=0).astype(copies.dtype)
    copies[...] = jnp.broadcast_to(rows[None], copies.shape)
    copies_out.start()
    copies_out.wait()
    keys_in.wait()


def dot_rows(a, b):
    return lax.dot_general(a, b, (((1,), (1,)), ((), ())), preferred_element_type=jnp.float32)


def side_by_side(first, second):
    zero = jnp.zeros_like(first)
    rows = [jnp.concatenate([first, zero], axis=1), jnp.concatenate([zero, second], axis=1)]
    return jnp.concatenate(rows, axis=0).astype(jnp.bfloat16)


def in_lanes(columns, rows):
    lane = lax.broadcasted_iota(jnp.int32, (rows, HEAD_DIM), 1)
    out = jnp.zeros((rows, HEAD_DIM), jnp.float32)
    for j, column in enumerate(columns):
        out = jnp.where(lane == j, column, out)
    return out


def own_kernel(
    lengths_ref, copies_ref, own_key_ref, own_value_ref, value_ref,
    own_ref, sums_ref, value_out,
    length, query_buf, own_key, own_value, sems,
):
    moves = (
        (copies_ref.at[0], query_buf),
        (own_key_ref, own_key),
        (lengths_ref, length),
        (own_value_ref, own_value),
        (value_ref, value_out),
    )
    moves = [pltpu.make_async_copy(a, b, sems.at[i]) for i, (a, b) in enumerate(moves)]
    for move in moves:
        move.start()
    span = own_key.shape[0]
    position = lax.broadcasted_iota(jnp.int32, (2 * GROUP, span), 1) + lax.axis_index("grp") * span
    moves[0].wait()
    query = query_buf[...].astype(jnp.float32)
    moves[1].wait()
    scores = []
    for i in range(PAIRS):
        top = 2 * i * GROUP
        both = side_by_side(query[top : top + GROUP], query[top + GROUP : top + 2 * GROUP])
        scores.append(dot_rows(both, own_key[:, i * PAIR_DIM : (i + 1) * PAIR_DIM]))
    moves[2].wait()
    live = position < length[...]
    moves[3].wait()
    peaks, totals = [], []
    for i in range(PAIRS):
        masked = jnp.where(live, scores[i], LOWEST)
        peak = jnp.max(masked, axis=1, keepdims=True)
        expo = jnp.where(live, jnp.exp((masked - peak) * SCALE), 0.0)
        total = jnp.sum(expo, axis=1, keepdims=True)
        output = jnp.dot(
            expo.astype(jnp.bfloat16),
            own_value[:, i * PAIR_DIM : (i + 1) * PAIR_DIM],
            preferred_element_type=jnp.float32,
        )
        own_ref[2 * i] = output[:GROUP, :HEAD_DIM]
        own_ref[2 * i + 1] = output[GROUP:, HEAD_DIM:]
        peaks += [peak[:GROUP], peak[GROUP:]]
        totals += [total[:GROUP], total[GROUP:]]
    sums_ref[0] = in_lanes(peaks, GROUP)
    sums_ref[1] = in_lanes(totals, GROUP)
    moves[4].wait()


def partial_kernel(query_ref, key_ref, value_ref, own_ref, own_sums_ref, out_ref, sums_ref):
    count = query_ref.shape[0]
    me = lax.axis_index("seq")
    chunks = out_ref.reshape(out_ref.shape[0] * ROWS, HEAD_DIM)

    def join_own():
        row = (me % BLOCK) * GROUP
        peak, total = sums_ref[pl.ds(row, GROUP)], sums_ref[pl.ds(BLOCK_ROWS + row, GROUP)]
        own_peak, own_total = own_sums_ref[0], own_sums_ref[1]
        joined = jnp.maximum(peak, own_peak)
        factor = jnp.exp((peak - joined) * SCALE)
        own_factor = jnp.exp((own_peak - joined) * SCALE)
        sums_ref[pl.ds(row, GROUP)] = joined
        sums_ref[pl.ds(BLOCK_ROWS + row, GROUP)] = total * factor + own_total * own_factor
        for j in range(KV_HEADS):
            rows = pl.ds((me * KV_HEADS + j) * ROWS, GROUP)
            chunks[rows] = chunks[rows] * factor[:, j : j + 1] + own_ref[j] * own_factor[:, j : j + 1]

    def one_block(block):
        queries = query_ref[pl.ds(block * BLOCK, BLOCK)].astype(jnp.float32)
        heads = [
            queries[:, j * GROUP : (j + 1) * GROUP].reshape(BLOCK_ROWS, HEAD_DIM)
            for j in range(KV_HEADS)
        ]
        scores = [
            dot_rows(
                side_by_side(heads[2 * i], heads[2 * i + 1]),
                key_ref[:, i * PAIR_DIM : (i + 1) * PAIR_DIM],
            )
            for i in range(PAIRS)
        ]
        peaks, totals = [], []
        for i in range(PAIRS):
            peak = jnp.max(scores[i], axis=1, keepdims=True)
            expo = jnp.exp((scores[i] - peak) * SCALE)
            total = jnp.sum(expo, axis=1, keepdims=True)
            output = jnp.dot(
                expo.astype(jnp.bfloat16),
                value_ref[:, i * PAIR_DIM : (i + 1) * PAIR_DIM],
                preferred_element_type=jnp.float32,
            )
            for r in range(BLOCK):
                for h in range(2):
                    rows = slice(h * BLOCK_ROWS + r * GROUP, h * BLOCK_ROWS + (r + 1) * GROUP)
                    chunk = ((block * BLOCK + r) * KV_HEADS + 2 * i + h) * ROWS
                    chunks[pl.ds(chunk, GROUP)] = output[rows, h * HEAD_DIM : (h + 1) * HEAD_DIM]
            peaks += [peak[:BLOCK_ROWS], peak[BLOCK_ROWS:]]
            totals += [total[:BLOCK_ROWS], total[BLOCK_ROWS:]]
        sums_ref[:BLOCK_ROWS] = in_lanes(peaks, BLOCK_ROWS)
        sums_ref[BLOCK_ROWS:] = in_lanes(totals, BLOCK_ROWS)
        if count == BLOCK:
            join_own()
        else:
            pl.when(me // BLOCK == block)(join_own)
        sums = sums_ref[...].T
        for r in range(BLOCK):
            for j in range(KV_HEADS):
                chunk = ((block * BLOCK + r) * KV_HEADS + j) * ROWS
                chunks[pl.ds(chunk + GROUP, 1)] = sums[j : j + 1]

    if count == BLOCK:
        one_block(0)
    else:
        pl.loop(0, count // BLOCK)(one_block)


def join_kernel(parts_ref, out_ref):
    sums = parts_ref[:, 0, GROUP * HEAD_DIM :]
    offset = (lax.axis_index("seq") % BLOCK) * GROUP
    peaks = pltpu.roll(sums, (HEAD_DIM - offset) % HEAD_DIM, 1)
    totals = pltpu.roll(peaks, HEAD_DIM - BLOCK_ROWS, 1)
    factor = jnp.exp((peaks - jnp.max(peaks, axis=0, keepdims=True)) * SCALE)
    factor = factor / jnp.sum(factor * totals, axis=0, keepdims=True)
    for h in range(GROUP):
        columns = slice(h * HEAD_DIM, (h + 1) * HEAD_DIM)
        output = jnp.sum(parts_ref[:, 0, columns] * factor[:, h : h + 1], axis=0, keepdims=True)
        out_ref[:, columns] = output.astype(out_ref.dtype)


def on_device(seq, grp, queries, prompt_keys, prompt_values, suffix_keys, suffix_values, lengths):
    copies, keys = pl.pallas_call(
        spread_kernel,
        out_shape=(
            jax.ShapeDtypeStruct((seq, Q_HEADS, HEAD_DIM), queries.dtype),
            pltpu.VMEM(prompt_keys.shape, prompt_keys.dtype),
        ),
        in_specs=[ANY] * 2,
        out_specs=(ANY, VMEM),
        scratch_shapes=[
            pltpu.VMEM(queries.shape, queries.dtype),
            pltpu.VMEM((seq, Q_HEADS, HEAD_DIM), queries.dtype),
            pltpu.SemaphoreType.DMA((3,)),
        ],
    )(queries, prompt_keys)
    every = lax.all_to_all(copies, "seq", 0, 0, tiled=True)
    span = suffix_keys.shape[1]
    width = KV_HEADS * HEAD_DIM
    own, own_sums, values = pl.pallas_call(
        own_kernel,
        out_shape=(
            pltpu.VMEM((KV_HEADS, GROUP, HEAD_DIM), jnp.float32),
            pltpu.VMEM((2, GROUP, HEAD_DIM), jnp.float32),
            pltpu.VMEM(prompt_values.shape, prompt_values.dtype),
        ),
        in_specs=[ANY] * 5,
        out_specs=(VMEM,) * 3,
        scratch_shapes=[
            pltpu.VMEM((1, 1), jnp.int32),
            pltpu.VMEM((Q_HEADS, HEAD_DIM), queries.dtype),
            pltpu.VMEM((span, width), suffix_keys.dtype),
            pltpu.VMEM((span, width), suffix_values.dtype),
            pltpu.SemaphoreType.DMA((5,)),
        ],
    )(
        lengths.reshape(1, 1),
        copies,
        suffix_keys.reshape(span, width),
        suffix_values.reshape(span, width),
        prompt_values,
    )
    partial = pl.pallas_call(
        partial_kernel,
        out_shape=pltpu.VMEM((seq * grp, 1, WIDTH), jnp.float32),
        in_specs=[VMEM] * 5,
        out_specs=VMEM,
        scratch_shapes=[pltpu.VMEM((2 * BLOCK_ROWS, HEAD_DIM), jnp.float32)],
    )(in_vmem(every), in_vmem(keys), in_vmem(values), in_vmem(own), in_vmem(own_sums))
    parts = lax.all_to_all(partial, ("seq", "grp"), 0, 0, tiled=True)
    return pl.pallas_call(
        join_kernel,
        out_shape=jax.ShapeDtypeStruct((1, GROUP * HEAD_DIM), queries.dtype),
        in_specs=[VMEM],
        out_specs=VMEM,
    )(in_vmem(parts))


def solution(mesh):
    in_specs = (
        P("seq", None),
        P(("seq", "grp"), None),
        P(("seq", "grp"), None),
        P("seq", "grp", None),
        P("seq", "grp", None),
        P("seq"),
    )
    return jax.shard_map(
        functools.partial(on_device, mesh.shape["seq"], mesh.shape["grp"]),
        mesh=mesh,
        in_specs=in_specs,
        out_specs=P("seq", "grp"),
        check_vma=False,
    )
```

```python
import functools
import math

import jax
import jax.numpy as jnp
from jax import lax
from jax.experimental import pallas as pl
from jax.experimental.pallas import tpu as pltpu
from jax.sharding import PartitionSpec as P

Q_HEADS = 32
KV_HEADS = 4
HEAD_DIM = 128
GROUP = 8
PAIRS = KV_HEADS // 2
PAIR_DIM = 2 * HEAD_DIM
BLOCK = 8
BLOCK_ROWS = BLOCK * GROUP
ROWS = GROUP + 2
SHARED = 2
DIRECT = ((5, 7), (3, 4), (1, 6))
COARSE = 8.0
SCALE = 1.0 / math.sqrt(HEAD_DIM)
LOWEST = -1e30
SMALLEST = 2.0**-120

VMEM = pl.BlockSpec(memory_space=pltpu.VMEM)
ANY = pl.BlockSpec(memory_space=pl.ANY)


def in_vmem(x):
    return pltpu.with_memory_space_constraint(x, pltpu.VMEM)


def head_rows(query_ref):
    row = query_ref[...].astype(jnp.float32)
    rows = [row[:, h * HEAD_DIM : (h + 1) * HEAD_DIM] for h in range(Q_HEADS)]
    return jnp.concatenate(rows, axis=0).astype(query_ref.dtype)


def spread_kernel(query_ref, out_ref):
    out_ref[...] = jnp.broadcast_to(head_rows(query_ref)[None], out_ref.shape)


def collect_kernel(own_ref, shared_ref, *refs):
    *direct_refs, near_ref, mine_ref = refs
    near_ref[0] = own_ref[...]
    near_ref[1] = head_rows(shared_ref)
    for i, ref in enumerate(direct_refs):
        mine_ref[i] = head_rows(ref)


def dot_rows(a, b):
    return lax.dot_general(a, b, (((1,), (1,)), ((), ())), preferred_element_type=jnp.float32)


def side_by_side(first, second):
    zero = jnp.zeros_like(first)
    rows = [jnp.concatenate([first, zero], axis=1), jnp.concatenate([zero, second], axis=1)]
    return jnp.concatenate(rows, axis=0).astype(jnp.bfloat16)


def in_lanes(columns, rows):
    lane = lax.broadcasted_iota(jnp.int32, (rows, HEAD_DIM), 1)
    out = jnp.zeros((rows, HEAD_DIM), jnp.float32)
    for j, column in enumerate(columns):
        out = jnp.where(lane == j, column, out)
    return out


def own_kernel(
    lengths_ref, query_ref, own_key_ref, own_value_ref, key_ref, value_ref,
    own_ref, sums_ref, rows_ref, key_out, value_out,
    length, query_buf, own_key, own_value, sems,
):
    moves = (
        (query_ref, query_buf),
        (own_key_ref, own_key),
        (lengths_ref, length),
        (own_value_ref, own_value),
        (value_ref, value_out),
        (key_ref, key_out),
    )
    moves = [pltpu.make_async_copy(a, b, sems.at[i]) for i, (a, b) in enumerate(moves)]
    for move in moves:
        move.start()
    span = own_key.shape[0]
    position = lax.broadcasted_iota(jnp.int32, (2 * GROUP, span), 1) + lax.axis_index("grp") * span
    moves[0].wait()
    rows_ref[...] = head_rows(query_buf)
    query = rows_ref[...].astype(jnp.float32)
    moves[1].wait()
    scores = []
    for i in range(PAIRS):
        top = 2 * i * GROUP
        both = side_by_side(query[top : top + GROUP], query[top + GROUP : top + 2 * GROUP])
        scores.append(dot_rows(both, own_key[:, i * PAIR_DIM : (i + 1) * PAIR_DIM]))
    moves[2].wait()
    live = position < length[...]
    moves[3].wait()
    peaks, totals = [], []
    for i in range(PAIRS):
        masked = jnp.where(live, scores[i], LOWEST)
        peak = jnp.max(masked, axis=1, keepdims=True)
        expo = jnp.where(live, jnp.exp((masked - peak) * SCALE), 0.0)
        total = jnp.sum(expo, axis=1, keepdims=True)
        output = jnp.dot(
            expo.astype(jnp.bfloat16),
            own_value[:, i * PAIR_DIM : (i + 1) * PAIR_DIM],
            preferred_element_type=jnp.float32,
        )
        own_ref[2 * i] = output[:GROUP, :HEAD_DIM]
        own_ref[2 * i + 1] = output[GROUP:, HEAD_DIM:]
        peaks += [peak[:GROUP], peak[GROUP:]]
        totals += [total[:GROUP], total[GROUP:]]
    largest = jnp.max(jnp.abs(own_value[...]), axis=0, keepdims=True)
    moves[4].wait()
    largest = jnp.maximum(largest, jnp.max(jnp.abs(value_out[...]), axis=0, keepdims=True))
    largest = jnp.max(largest.astype(jnp.float32), axis=1, keepdims=True)
    power = jnp.ceil(jnp.log2(jnp.maximum(largest, SMALLEST)))
    power -= 15 - (key_ref.shape[0] + span - 1).bit_length()
    shrink = jnp.exp2(-power)
    for j in range(KV_HEADS):
        own_ref[j] *= shrink
    sums_ref[0] = in_lanes(peaks, GROUP)
    sums_ref[1] = in_lanes(totals, GROUP)
    sums_ref[2] = jnp.broadcast_to(power * (math.log(2.0) / SCALE), (GROUP, HEAD_DIM))
    sums_ref[3] = jnp.broadcast_to(shrink, (GROUP, HEAD_DIM))
    moves[5].wait()


def partial_kernel(
    gathered, key_ref, value_ref, own_ref, own_sums_ref, *refs
):
    me = lax.axis_index("seq")
    if gathered:
        query_ref, out_ref, sums_ref = refs
    else:
        near_ref, mine_ref, other_ref, out_ref, sums_ref, query_ref = refs
        core = lax.axis_index("grp") % 2
        query_ref[me] = near_ref[0]
        query_ref[me ^ SHARED] = near_ref[1]
        for i, (even, odd) in enumerate(DIRECT):
            query_ref[me ^ jnp.where(core == 0, even, odd)] = mine_ref[i]
            query_ref[me ^ jnp.where(core == 0, odd, even)] = other_ref[i]
    count = query_ref.shape[0]
    shrink = own_sums_ref[3, :1, :1]

    def columns(i):
        return slice(i * HEAD_DIM, (i + 1) * HEAD_DIM)

    def join_own():
        row = (me % BLOCK) * GROUP
        peak, total = sums_ref[pl.ds(row, GROUP)], sums_ref[pl.ds(BLOCK_ROWS + row, GROUP)]
        own_peak, own_total = own_sums_ref[0], own_sums_ref[1]
        joined = jnp.maximum(peak, own_peak)
        factor = jnp.exp((peak - joined) * SCALE)
        own_factor = jnp.exp((own_peak - joined) * SCALE)
        sums_ref[pl.ds(row, GROUP)] = joined
        sums_ref[pl.ds(BLOCK_ROWS + row, GROUP)] = total * factor + own_total * own_factor
        for j in range(KV_HEADS):
            rows = pl.ds((me * KV_HEADS + j) * ROWS, GROUP)
            out_ref[rows] = out_ref[rows] * factor[:, j : j + 1] + own_ref[j] * own_factor[:, j : j + 1]

    def one_block(block):
        queries = query_ref[pl.ds(block * BLOCK, BLOCK)].astype(jnp.float32)
        heads = [
            queries[:, j * GROUP : (j + 1) * GROUP].reshape(BLOCK_ROWS, HEAD_DIM)
            for j in range(KV_HEADS)
        ]
        scores = [
            dot_rows(
                side_by_side(heads[2 * i], heads[2 * i + 1]),
                key_ref[:, i * PAIR_DIM : (i + 1) * PAIR_DIM],
            )
            for i in range(PAIRS)
        ]
        peaks, totals = [], []
        for i in range(PAIRS):
            peak = jnp.max(scores[i], axis=1, keepdims=True)
            expo = jnp.exp((scores[i] - peak) * SCALE)
            total = jnp.sum(expo, axis=1, keepdims=True)
            output = jnp.dot(
                expo.astype(jnp.bfloat16),
                value_ref[:, i * PAIR_DIM : (i + 1) * PAIR_DIM],
                preferred_element_type=jnp.float32,
            )
            for r in range(BLOCK):
                for h in range(2):
                    rows = slice(h * BLOCK_ROWS + r * GROUP, h * BLOCK_ROWS + (r + 1) * GROUP)
                    chunk = ((block * BLOCK + r) * KV_HEADS + 2 * i + h) * ROWS
                    out_ref[pl.ds(chunk, GROUP)] = output[rows, columns(h)] * shrink
            peaks += [peak[:BLOCK_ROWS], peak[BLOCK_ROWS:]]
            totals += [total[:BLOCK_ROWS], total[BLOCK_ROWS:]]
        sums_ref[:BLOCK_ROWS] = in_lanes(peaks, BLOCK_ROWS)
        sums_ref[BLOCK_ROWS:] = in_lanes(totals, BLOCK_ROWS)
        if count == BLOCK:
            join_own()
        else:
            pl.when(me // BLOCK == block)(join_own)
        sums = sums_ref[...].T[:GROUP]
        lane = lax.broadcasted_iota(jnp.int32, (GROUP, HEAD_DIM), 1)
        peaks = jnp.where(lane < BLOCK_ROWS, sums, pltpu.roll(sums, BLOCK_ROWS, 1))
        weights = peaks + jnp.where(
            lane < BLOCK_ROWS, own_sums_ref[2], jnp.log(sums) * (1.0 / SCALE)
        )
        coarse = jnp.round(weights * (1.0 / COARSE)) * COARSE
        fine = weights - coarse
        for r in range(BLOCK):
            for j in range(KV_HEADS):
                chunk = ((block * BLOCK + r) * KV_HEADS + j) * ROWS
                out_ref[pl.ds(chunk + GROUP, 1)] = coarse[j : j + 1]
                out_ref[pl.ds(chunk + GROUP + 1, 1)] = fine[j : j + 1]

    if count == BLOCK:
        one_block(0)
    else:
        pl.loop(0, count // BLOCK)(one_block)


def join_kernel(parts_ref, out_ref):
    parts = parts_ref.shape[0] // ROWS

    def every(row):
        return parts_ref[pl.ds(row, parts, stride=ROWS)]

    offset = (lax.axis_index("seq") % BLOCK) * GROUP
    weights = pltpu.roll(every(GROUP) + every(GROUP + 1), (HEAD_DIM - offset) % HEAD_DIM, 1)
    totals = pltpu.roll(weights, HEAD_DIM - BLOCK_ROWS, 1)
    top = jnp.max(totals, axis=0, keepdims=True)
    total = jnp.sum(jnp.exp((totals - top) * SCALE), axis=0, keepdims=True)
    factor = jnp.exp((weights - top) * SCALE) / total
    for h in range(GROUP):
        output = jnp.sum(every(h) * factor[:, h : h + 1], axis=0, keepdims=True)
        out_ref[:, h * HEAD_DIM : (h + 1) * HEAD_DIM] = output.astype(out_ref.dtype)


def straight(seq, grp, even, odd):
    return [
        (i * grp + j, (i ^ (odd if j % 2 else even)) * grp + j) for i in range(seq) for j in range(grp)
    ]


def on_device(seq, grp, queries, prompt_keys, prompt_values, suffix_keys, suffix_values, lengths):
    span = suffix_keys.shape[1]
    width = KV_HEADS * HEAD_DIM
    own, own_sums, rows, keys, values = pl.pallas_call(
        own_kernel,
        out_shape=(
            pltpu.VMEM((KV_HEADS, GROUP, HEAD_DIM), jnp.float32),
            pltpu.VMEM((4, GROUP, HEAD_DIM), jnp.float32),
            pltpu.VMEM((Q_HEADS, HEAD_DIM), queries.dtype),
            pltpu.VMEM(prompt_keys.shape, prompt_keys.dtype),
            pltpu.VMEM(prompt_values.shape, prompt_values.dtype),
        ),
        in_specs=[ANY] * 6,
        out_specs=(VMEM,) * 5,
        scratch_shapes=[
            pltpu.VMEM((1, 1), jnp.int32),
            pltpu.VMEM(queries.shape, queries.dtype),
            pltpu.VMEM((span, width), suffix_keys.dtype),
            pltpu.VMEM((span, width), suffix_values.dtype),
            pltpu.SemaphoreType.DMA((6,)),
        ],
    )(
        lengths.reshape(1, 1),
        queries,
        suffix_keys.reshape(span, width),
        suffix_values.reshape(span, width),
        prompt_keys,
        prompt_values,
    )
    scratch = [pltpu.VMEM((2 * BLOCK_ROWS, HEAD_DIM), jnp.float32)]
    if seq == BLOCK and grp % 2 == 0:
        direct = [
            lax.ppermute(queries, ("seq", "grp"), straight(seq, grp, even, odd)) for even, odd in DIRECT
        ]
        shared = lax.ppermute(queries, ("seq", "grp"), straight(seq, grp, SHARED, SHARED))
        near, mine = pl.pallas_call(
            collect_kernel,
            out_shape=(
                pltpu.VMEM((2, Q_HEADS, HEAD_DIM), queries.dtype),
                pltpu.VMEM((len(DIRECT), Q_HEADS, HEAD_DIM), queries.dtype),
            ),
            in_specs=[VMEM] * (2 + len(DIRECT)),
            out_specs=(VMEM, VMEM),
        )(in_vmem(rows), in_vmem(shared), *map(in_vmem, direct))
        other = lax.ppermute(mine, "grp", [(j, j ^ 1) for j in range(grp)])
        every = [near, mine, other]
        scratch.append(pltpu.VMEM((seq, Q_HEADS, HEAD_DIM), queries.dtype))
    else:
        copies = pl.pallas_call(
            spread_kernel,
            out_shape=pltpu.VMEM((seq, Q_HEADS, HEAD_DIM), queries.dtype),
            in_specs=[VMEM],
            out_specs=VMEM,
        )(queries)
        every = [lax.all_to_all(copies, "seq", 0, 0, tiled=True)]
    partial = pl.pallas_call(
        functools.partial(partial_kernel, len(every) == 1),
        out_shape=pltpu.VMEM((seq * grp * ROWS, HEAD_DIM), jnp.float32),
        in_specs=[VMEM] * (4 + len(every)),
        out_specs=VMEM,
        scratch_shapes=scratch,
    )(in_vmem(keys), in_vmem(values), in_vmem(own), in_vmem(own_sums), *map(in_vmem, every))
    partial = partial.reshape(seq * grp, ROWS // 2, 2, HEAD_DIM).astype(jnp.float16)
    parts = lax.all_to_all(partial, ("seq", "grp"), 0, 0, tiled=True)
    parts = parts.astype(jnp.float32).reshape(seq * grp * ROWS, HEAD_DIM)
    return pl.pallas_call(
        join_kernel,
        out_shape=jax.ShapeDtypeStruct((1, GROUP * HEAD_DIM), queries.dtype),
        in_specs=[VMEM],
        out_specs=VMEM,
    )(in_vmem(parts))


def solution(mesh):
    in_specs = (
        P("seq", None),
        P(("seq", "grp"), None),
        P(("seq", "grp"), None),
        P("seq", "grp", None),
        P("seq", "grp", None),
        P("seq"),
    )
    return jax.shard_map(
        functools.partial(on_device, mesh.shape["seq"], mesh.shape["grp"]),
        mesh=mesh,
        in_specs=in_specs,
        out_specs=P("seq", "grp"),
        check_vma=False,
    )
```

```python
import functools
import math

import jax
import jax.numpy as jnp
from jax import lax
from jax.experimental import pallas as pl
from jax.experimental.pallas import tpu as pltpu
from jax.sharding import PartitionSpec as P

Q_HEADS = 32
KV_HEADS = 4
HEAD_DIM = 128
GROUP = 8
PAIRS = KV_HEADS // 2
PAIR_DIM = 2 * HEAD_DIM
BLOCK = 8
BLOCK_ROWS = BLOCK * GROUP
ROWS = GROUP + 2
SHARED = 2
DIRECT = ((5, 7), (3, 4), (1, 6))
ORDER = (1, 0, 3, 2)
COARSE = 8.0
SCALE = 1.0 / math.sqrt(HEAD_DIM)
LOWEST = -1e30
LIMIT = pltpu.CompilerParams(vmem_limit_bytes=24 << 20)
SMALLEST = 2.0**-120

VMEM = pl.BlockSpec(memory_space=pltpu.VMEM)
HBM = pl.BlockSpec(memory_space=pltpu.HBM)
ANY = pl.BlockSpec(memory_space=pl.ANY)


def in_vmem(x):
    return pltpu.with_memory_space_constraint(x, pltpu.VMEM)


def in_hbm(x):
    return pltpu.with_memory_space_constraint(x, pltpu.HBM)


def head_rows(query_ref):
    row = query_ref[...].astype(jnp.float32)
    rows = [row[:, h * HEAD_DIM : (h + 1) * HEAD_DIM] for h in range(Q_HEADS)]
    return jnp.concatenate(rows, axis=0).astype(query_ref.dtype)


def spread_kernel(query_ref, out_ref):
    out_ref[...] = jnp.broadcast_to(head_rows(query_ref)[None], out_ref.shape)


def collect_kernel(own_ref, *refs):
    *in_refs, near_ref, mine_ref = refs
    near_ref[0] = own_ref[0]
    for i, ref in zip(ORDER, in_refs):
        if i == len(DIRECT):
            near_ref[1] = head_rows(ref)
        else:
            mine_ref[i] = head_rows(ref)


def dot_rows(a, b):
    return lax.dot_general(a, b, (((1,), (1,)), ((), ())), preferred_element_type=jnp.float32)


def side_by_side(first, second):
    zero = jnp.zeros_like(first)
    rows = [jnp.concatenate([first, zero], axis=1), jnp.concatenate([zero, second], axis=1)]
    return jnp.concatenate(rows, axis=0).astype(jnp.bfloat16)


def in_lanes(columns, rows):
    lane = lax.broadcasted_iota(jnp.int32, (rows, HEAD_DIM), 1)
    out = jnp.zeros((rows, HEAD_DIM), jnp.float32)
    for j, column in enumerate(columns):
        out = jnp.where(lane == j, column, out)
    return out


def load_kernel(
    query_ref, lengths_ref, own_key_ref, own_value_ref, key_ref, value_ref,
    rows_ref, length_ref, own_key_out, own_value_out, key_out, value_out,
    query, length, key, sems,
):
    moves = (
        (query_ref, query),
        (key_ref, key),
        (lengths_ref, length),
        (own_key_ref, own_key_out),
        (own_value_ref, own_value_out),
        (value_ref, value_out),
    )
    moves = [pltpu.make_async_copy(a, b, sems.at[i]) for i, (a, b) in enumerate(moves)]
    for move in moves:
        move.start()
    moves[0].wait()
    rows_ref[0] = head_rows(query)
    moves[1].wait()
    key_out[...] = key[...].T
    moves[2].wait()
    length_ref[...] = jnp.broadcast_to(length[...], length_ref.shape)
    for move in moves[3:]:
        move.wait()


def own_kernel(
    length_ref, query_ref, own_key_ref, own_value_ref, value_ref, own_ref, sums_ref
):
    span = own_key_ref.shape[0]
    position = lax.broadcasted_iota(jnp.int32, (2 * GROUP, span), 1) + lax.axis_index("grp") * span
    live = position < length_ref[:1, :1]
    query = query_ref[0].astype(jnp.float32)
    scores = []
    for i in range(PAIRS):
        top = 2 * i * GROUP
        both = side_by_side(query[top : top + GROUP], query[top + GROUP : top + 2 * GROUP])
        scores.append(dot_rows(both, own_key_ref[:, i * PAIR_DIM : (i + 1) * PAIR_DIM]))
    largest = jnp.max(jnp.abs(value_ref[...]), axis=0, keepdims=True)
    largest = jnp.maximum(largest, jnp.max(jnp.abs(own_value_ref[...]), axis=0, keepdims=True))
    largest = jnp.max(largest.astype(jnp.float32), axis=1, keepdims=True)
    power = jnp.ceil(jnp.log2(jnp.maximum(largest, SMALLEST)))
    power -= 15 - (value_ref.shape[0] + span - 1).bit_length()
    shrink = jnp.exp2(-power)
    peaks, totals = [], []
    for i in range(PAIRS):
        masked = jnp.where(live, scores[i], LOWEST)
        peak = jnp.max(masked, axis=1, keepdims=True)
        expo = jnp.where(live, jnp.exp((masked - peak) * SCALE), 0.0)
        total = jnp.sum(expo, axis=1, keepdims=True)
        output = jnp.dot(
            expo.astype(jnp.bfloat16),
            own_value_ref[:, i * PAIR_DIM : (i + 1) * PAIR_DIM],
            preferred_element_type=jnp.float32,
        )
        own_ref[2 * i] = output[:GROUP, :HEAD_DIM] * shrink
        own_ref[2 * i + 1] = output[GROUP:, HEAD_DIM:] * shrink
        peaks += [peak[:GROUP], peak[GROUP:]]
        totals += [total[:GROUP], total[GROUP:]]
    sums_ref[0] = in_lanes(peaks, GROUP)
    sums_ref[1] = in_lanes(totals, GROUP)
    sums_ref[2] = jnp.broadcast_to(power * (math.log(2.0) / SCALE), (GROUP, HEAD_DIM))
    sums_ref[3] = jnp.broadcast_to(shrink, (GROUP, HEAD_DIM))


def partial_kernel(
    gathered, key_ref, value_ref, own_ref, own_sums_ref, *refs
):
    me = lax.axis_index("seq")
    if gathered:
        query_ref, out_ref, sums_ref = refs
    else:
        near_ref, mine_ref, other_ref, out_ref, sums_ref, query_ref = refs
        core = lax.axis_index("grp") % 2
        query_ref[me] = near_ref[0]
        query_ref[me ^ SHARED] = near_ref[1]
        for i, (even, odd) in enumerate(DIRECT):
            query_ref[me ^ jnp.where(core == 0, even, odd)] = mine_ref[i]
            query_ref[me ^ jnp.where(core == 0, odd, even)] = other_ref[i]
    count = query_ref.shape[0]
    shrink = own_sums_ref[3, :1, :1]

    def columns(i):
        return slice(i * HEAD_DIM, (i + 1) * HEAD_DIM)

    def join_own():
        row = (me % BLOCK) * GROUP
        peak, total = sums_ref[pl.ds(row, GROUP)], sums_ref[pl.ds(BLOCK_ROWS + row, GROUP)]
        own_peak, own_total = own_sums_ref[0], own_sums_ref[1]
        joined = jnp.maximum(peak, own_peak)
        factor = jnp.exp((peak - joined) * SCALE)
        own_factor = jnp.exp((own_peak - joined) * SCALE)
        sums_ref[pl.ds(row, GROUP)] = joined
        sums_ref[pl.ds(BLOCK_ROWS + row, GROUP)] = total * factor + own_total * own_factor
        for j in range(KV_HEADS):
            rows = pl.ds((me * KV_HEADS + j) * ROWS, GROUP)
            out_ref[rows] = out_ref[rows] * factor[:, j : j + 1] + own_ref[j] * own_factor[:, j : j + 1]

    def one_block(block):
        queries = query_ref[pl.ds(block * BLOCK, BLOCK)].astype(jnp.float32)
        heads = [
            queries[:, j * GROUP : (j + 1) * GROUP].reshape(BLOCK_ROWS, HEAD_DIM)
            for j in range(KV_HEADS)
        ]
        scores = [
            jnp.dot(
                side_by_side(heads[2 * i], heads[2 * i + 1]),
                key_ref[i * PAIR_DIM : (i + 1) * PAIR_DIM],
                preferred_element_type=jnp.float32,
            )
            for i in range(PAIRS)
        ]
        peaks, totals = [], []
        for i in range(PAIRS):
            peak = jnp.max(scores[i], axis=1, keepdims=True)
            expo = jnp.exp((scores[i] - peak) * SCALE)
            total = jnp.sum(expo, axis=1, keepdims=True)
            output = jnp.dot(
                expo.astype(jnp.bfloat16),
                value_ref[:, i * PAIR_DIM : (i + 1) * PAIR_DIM],
                preferred_element_type=jnp.float32,
            )
            for r in range(BLOCK):
                for h in range(2):
                    rows = slice(h * BLOCK_ROWS + r * GROUP, h * BLOCK_ROWS + (r + 1) * GROUP)
                    chunk = ((block * BLOCK + r) * KV_HEADS + 2 * i + h) * ROWS
                    out_ref[pl.ds(chunk, GROUP)] = output[rows, columns(h)] * shrink
            peaks += [peak[:BLOCK_ROWS], peak[BLOCK_ROWS:]]
            totals += [total[:BLOCK_ROWS], total[BLOCK_ROWS:]]
        sums_ref[:BLOCK_ROWS] = in_lanes(peaks, BLOCK_ROWS)
        sums_ref[BLOCK_ROWS:] = in_lanes(totals, BLOCK_ROWS)
        if count == BLOCK:
            join_own()
        else:
            pl.when(me // BLOCK == block)(join_own)
        sums = sums_ref[...].T[:GROUP]
        lane = lax.broadcasted_iota(jnp.int32, (GROUP, HEAD_DIM), 1)
        peaks = jnp.where(lane < BLOCK_ROWS, sums, pltpu.roll(sums, BLOCK_ROWS, 1))
        weights = peaks + jnp.where(
            lane < BLOCK_ROWS, own_sums_ref[2], jnp.log(sums) * (1.0 / SCALE)
        )
        coarse = jnp.round(weights * (1.0 / COARSE)) * COARSE
        fine = weights - coarse
        for r in range(BLOCK):
            for j in range(KV_HEADS):
                chunk = ((block * BLOCK + r) * KV_HEADS + j) * ROWS
                out_ref[pl.ds(chunk + GROUP, 1)] = coarse[j : j + 1]
                out_ref[pl.ds(chunk + GROUP + 1, 1)] = fine[j : j + 1]

    if count == BLOCK:
        one_block(0)
    else:
        pl.loop(0, count // BLOCK)(one_block)


def join_kernel(parts_ref, out_ref):
    parts = parts_ref.shape[0] // ROWS

    def every(row):
        return parts_ref[pl.ds(row, parts, stride=ROWS)]

    offset = (lax.axis_index("seq") % BLOCK) * GROUP
    weights = pltpu.roll(every(GROUP) + every(GROUP + 1), (HEAD_DIM - offset) % HEAD_DIM, 1)
    totals = pltpu.roll(weights, HEAD_DIM - BLOCK_ROWS, 1)
    top = jnp.max(totals, axis=0, keepdims=True)
    total = jnp.sum(jnp.exp((totals - top) * SCALE), axis=0, keepdims=True)
    factor = jnp.exp((weights - top) * SCALE) / total
    for h in range(GROUP):
        output = jnp.sum(every(h) * factor[:, h : h + 1], axis=0, keepdims=True)
        out_ref[:, h * HEAD_DIM : (h + 1) * HEAD_DIM] = output.astype(out_ref.dtype)


def straight(seq, grp, even, odd):
    return [
        (i * grp + j, (i ^ (odd if j % 2 else even)) * grp + j) for i in range(seq) for j in range(grp)
    ]


def on_device(seq, grp, queries, prompt_keys, prompt_values, suffix_keys, suffix_values, lengths):
    span = suffix_keys.shape[1]
    width = KV_HEADS * HEAD_DIM
    rows, length, own_keys, own_values, keys, values = pl.pallas_call(
        load_kernel,
        compiler_params=LIMIT,
        out_shape=(
            pltpu.VMEM((1, Q_HEADS, HEAD_DIM), queries.dtype),
            pltpu.VMEM((GROUP, HEAD_DIM), jnp.int32),
            pltpu.VMEM((span, width), suffix_keys.dtype),
            pltpu.VMEM((span, width), suffix_values.dtype),
            pltpu.VMEM(prompt_keys.shape[::-1], prompt_keys.dtype),
            pltpu.VMEM(prompt_values.shape, prompt_values.dtype),
        ),
        in_specs=[HBM, ANY] + [HBM] * 4,
        out_specs=(VMEM,) * 6,
        scratch_shapes=[
            pltpu.VMEM(queries.shape, queries.dtype),
            pltpu.VMEM((1, 1), jnp.int32),
            pltpu.VMEM(prompt_keys.shape, prompt_keys.dtype),
            pltpu.SemaphoreType.DMA((6,)),
        ],
    )(
        in_hbm(queries),
        lengths.reshape(1, 1),
        in_hbm(suffix_keys.reshape(span, width)),
        in_hbm(suffix_values.reshape(span, width)),
        in_hbm(prompt_keys),
        in_hbm(prompt_values),
    )
    scratch = [pltpu.VMEM((2 * BLOCK_ROWS, HEAD_DIM), jnp.float32)]
    if seq == BLOCK and grp % 2 == 0:
        direct = [
            lax.ppermute(queries, ("seq", "grp"), straight(seq, grp, even, odd)) for even, odd in DIRECT
        ]
        shared = lax.ppermute(queries, ("seq", "grp"), straight(seq, grp, SHARED, SHARED))
        near, mine = pl.pallas_call(
            collect_kernel,
            compiler_params=LIMIT,
            out_shape=(
                pltpu.VMEM((2, Q_HEADS, HEAD_DIM), queries.dtype),
                pltpu.VMEM((len(DIRECT), Q_HEADS, HEAD_DIM), queries.dtype),
            ),
            in_specs=[VMEM] * (2 + len(DIRECT)),
            out_specs=(VMEM, VMEM),
        )(in_vmem(rows), *[in_vmem([*direct, shared][i]) for i in ORDER])
        other = lax.ppermute(mine, "grp", [(j, j ^ 1) for j in range(grp)])
        own_rows, every = near, [near, mine, other]
        scratch.append(pltpu.VMEM((seq, Q_HEADS, HEAD_DIM), queries.dtype))
    else:
        copies = pl.pallas_call(
            spread_kernel,
            compiler_params=LIMIT,
            out_shape=pltpu.VMEM((seq, Q_HEADS, HEAD_DIM), queries.dtype),
            in_specs=[VMEM],
            out_specs=VMEM,
        )(queries)
        own_rows, every = rows, [lax.all_to_all(copies, "seq", 0, 0, tiled=True)]
    own, own_sums = pl.pallas_call(
        own_kernel,
        compiler_params=LIMIT,
        out_shape=(
            pltpu.VMEM((KV_HEADS, GROUP, HEAD_DIM), jnp.float32),
            pltpu.VMEM((4, GROUP, HEAD_DIM), jnp.float32),
        ),
        in_specs=[VMEM] * 5,
        out_specs=(VMEM, VMEM),
    )(*map(in_vmem, (length, own_rows, own_keys, own_values, values)))
    partial = pl.pallas_call(
        functools.partial(partial_kernel, len(every) == 1),
        compiler_params=LIMIT,
        out_shape=pltpu.VMEM((seq * grp * ROWS, HEAD_DIM), jnp.float32),
        in_specs=[VMEM] * (4 + len(every)),
        out_specs=VMEM,
        scratch_shapes=scratch,
    )(in_vmem(keys), in_vmem(values), in_vmem(own), in_vmem(own_sums), *map(in_vmem, every))
    partial = partial.reshape(seq * grp, ROWS // 2, 2, HEAD_DIM).astype(jnp.float16)
    parts = lax.all_to_all(partial, ("seq", "grp"), 0, 0, tiled=True)
    parts = parts.astype(jnp.float32).reshape(seq * grp * ROWS, HEAD_DIM)
    return pl.pallas_call(
        join_kernel,
        compiler_params=LIMIT,
        out_shape=jax.ShapeDtypeStruct((1, GROUP * HEAD_DIM), queries.dtype),
        in_specs=[VMEM],
        out_specs=VMEM,
    )(in_vmem(parts))


def solution(mesh):
    in_specs = (
        P("seq", None),
        P(("seq", "grp"), None),
        P(("seq", "grp"), None),
        P("seq", "grp", None),
        P("seq", "grp", None),
        P("seq"),
    )
    return jax.shard_map(
        functools.partial(on_device, mesh.shape["seq"], mesh.shape["grp"]),
        mesh=mesh,
        in_specs=in_specs,
        out_specs=P("seq", "grp"),
        check_vma=False,
    )
```

```python
import functools
import math

import jax
import jax.numpy as jnp
from jax import lax
from jax.experimental import pallas as pl
from jax.experimental.pallas import tpu as pltpu
from jax.sharding import PartitionSpec as P

Q_HEADS = 32
KV_HEADS = 4
HEAD_DIM = 128
GROUP = 8
PAIRS = KV_HEADS // 2
PAIR_DIM = 2 * HEAD_DIM
BLOCK = 8
BLOCK_ROWS = BLOCK * GROUP
ROWS = GROUP + 2
SHARED = 2
DIRECT = ((5, 7), (3, 4), (1, 6))
ORDER = (1, 0, 3, 2)
COARSE = 8.0
SCALE = 1.0 / math.sqrt(HEAD_DIM)
LOWEST = -1e30
LIMIT = pltpu.CompilerParams(vmem_limit_bytes=24 << 20)
SMALLEST = 2.0**-120

VMEM = pl.BlockSpec(memory_space=pltpu.VMEM)
HBM = pl.BlockSpec(memory_space=pltpu.HBM)
ANY = pl.BlockSpec(memory_space=pl.ANY)


def in_vmem(x):
    return pltpu.with_memory_space_constraint(x, pltpu.VMEM)


def in_hbm(x):
    return pltpu.with_memory_space_constraint(x, pltpu.HBM)


def head_rows(query_ref):
    row = query_ref[...].astype(jnp.float32)
    rows = [row[:, h * HEAD_DIM : (h + 1) * HEAD_DIM] for h in range(Q_HEADS)]
    return jnp.concatenate(rows, axis=0).astype(query_ref.dtype)


def spread_kernel(query_ref, out_ref):
    out_ref[...] = jnp.broadcast_to(head_rows(query_ref)[None], out_ref.shape)


def collect_kernel(own_ref, *refs):
    *in_refs, near_ref, mine_ref = refs
    near_ref[0] = own_ref[0]
    for i, ref in zip(ORDER, in_refs):
        if i == len(DIRECT):
            near_ref[1] = head_rows(ref)
        else:
            mine_ref[i] = head_rows(ref)


def dot_rows(a, b):
    return lax.dot_general(a, b, (((1,), (1,)), ((), ())), preferred_element_type=jnp.float32)


def side_by_side(first, second):
    zero = jnp.zeros_like(first)
    rows = [jnp.concatenate([first, zero], axis=1), jnp.concatenate([zero, second], axis=1)]
    return jnp.concatenate(rows, axis=0).astype(jnp.bfloat16)


def in_lanes(columns, rows):
    lane = lax.broadcasted_iota(jnp.int32, (rows, HEAD_DIM), 1)
    out = jnp.zeros((rows, HEAD_DIM), jnp.float32)
    for j, column in enumerate(columns):
        out = jnp.where(lane == j, column, out)
    return out


def both_halves(sums):
    lane = lax.broadcasted_iota(jnp.int32, sums.shape, 1)
    return jnp.where(lane < BLOCK_ROWS, sums, pltpu.roll(sums, BLOCK_ROWS, 1))


def load_kernel(
    query_ref, lengths_ref, own_key_ref, own_value_ref, key_ref, value_ref,
    rows_ref, length_ref, own_key_out, own_value_out, key_out, value_out,
    query, length, key, sems,
):
    moves = (
        (query_ref, query),
        (key_ref, key),
        (lengths_ref, length),
        (own_key_ref, own_key_out),
        (own_value_ref, own_value_out),
        (value_ref, value_out),
    )
    moves = [pltpu.make_async_copy(a, b, sems.at[i]) for i, (a, b) in enumerate(moves)]
    for move in moves:
        move.start()
    moves[0].wait()
    rows_ref[0] = head_rows(query)
    moves[1].wait()
    key_out[...] = key[...].T
    moves[2].wait()
    length_ref[...] = jnp.broadcast_to(length[...], length_ref.shape)
    for move in moves[3:]:
        move.wait()


def own_kernel(
    length_ref, query_ref, own_key_ref, own_value_ref, value_ref, own_ref, sums_ref, flat_ref, wide_ref
):
    span = own_key_ref.shape[0]
    position = lax.broadcasted_iota(jnp.int32, (2 * GROUP, span), 1) + lax.axis_index("grp") * span
    live = position < length_ref[:1, :1]
    query = query_ref[0].astype(jnp.float32)
    scores = []
    for i in range(PAIRS):
        top = 2 * i * GROUP
        both = side_by_side(query[top : top + GROUP], query[top + GROUP : top + 2 * GROUP])
        scores.append(dot_rows(both, own_key_ref[:, i * PAIR_DIM : (i + 1) * PAIR_DIM]))
    largest = jnp.max(jnp.abs(value_ref[...]), axis=0, keepdims=True)
    largest = jnp.maximum(largest, jnp.max(jnp.abs(own_value_ref[...]), axis=0, keepdims=True))
    largest = jnp.max(largest.astype(jnp.float32), axis=1, keepdims=True)
    power = jnp.ceil(jnp.log2(jnp.maximum(largest, SMALLEST)))
    power -= 15 - (value_ref.shape[0] + span - 1).bit_length()
    shrink = jnp.exp2(-power)
    peaks, totals = [], []
    for i in range(PAIRS):
        masked = jnp.where(live, scores[i], LOWEST)
        peak = jnp.max(masked, axis=1, keepdims=True)
        expo = jnp.where(live, jnp.exp((masked - peak) * SCALE), 0.0)
        total = jnp.sum(expo, axis=1, keepdims=True)
        output = jnp.dot(
            expo.astype(jnp.bfloat16),
            own_value_ref[:, i * PAIR_DIM : (i + 1) * PAIR_DIM],
            preferred_element_type=jnp.float32,
        )
        own_ref[2 * i] = output[:GROUP, :HEAD_DIM] * shrink
        own_ref[2 * i + 1] = output[GROUP:, HEAD_DIM:] * shrink
        peaks += [peak[:GROUP], peak[GROUP:]]
        totals += [total[:GROUP], total[GROUP:]]
    sums_ref[0] = in_lanes(peaks, GROUP)
    sums_ref[1] = in_lanes(totals, GROUP)
    sums_ref[2] = jnp.broadcast_to(power * (math.log(2.0) / SCALE), (GROUP, HEAD_DIM))
    sums_ref[3] = jnp.broadcast_to(shrink, (GROUP, HEAD_DIM))
    row = (lax.axis_index("seq") % BLOCK) * GROUP
    wide_ref[:BLOCK_ROWS] = jnp.full((BLOCK_ROWS, HEAD_DIM), LOWEST, jnp.float32)
    wide_ref[BLOCK_ROWS:] = jnp.zeros((BLOCK_ROWS, HEAD_DIM), jnp.float32)
    wide_ref[pl.ds(row, GROUP)] = sums_ref[0]
    wide_ref[pl.ds(BLOCK_ROWS + row, GROUP)] = sums_ref[1]
    flat_ref[0] = wide_ref[...].T[:GROUP]
    flat_ref[1] = both_halves(flat_ref[0])


def partial_kernel(
    gathered, key_ref, value_ref, own_ref, own_sums_ref, own_flat_ref, *refs
):
    me = lax.axis_index("seq")
    if gathered:
        query_ref, out_ref, sums_ref = refs
    else:
        near_ref, mine_ref, other_ref, out_ref, sums_ref, query_ref = refs
        core = lax.axis_index("grp") % 2
        query_ref[me] = near_ref[0]
        query_ref[me ^ SHARED] = near_ref[1]
        for i, (even, odd) in enumerate(DIRECT):
            query_ref[me ^ jnp.where(core == 0, even, odd)] = mine_ref[i]
            query_ref[me ^ jnp.where(core == 0, odd, even)] = other_ref[i]
    count = query_ref.shape[0]
    shrink = own_sums_ref[3, :1, :1]

    def columns(i):
        return slice(i * HEAD_DIM, (i + 1) * HEAD_DIM)

    def join_own():
        row = (me % BLOCK) * GROUP
        peak, own_peak = sums_ref[pl.ds(row, GROUP)], own_sums_ref[0]
        joined = jnp.maximum(peak, own_peak)
        factor = jnp.exp((peak - joined) * SCALE)
        own_factor = jnp.exp((own_peak - joined) * SCALE)
        for j in range(KV_HEADS):
            rows = pl.ds((me * KV_HEADS + j) * ROWS, GROUP)
            out_ref[rows] = out_ref[rows] * factor[:, j : j + 1] + own_ref[j] * own_factor[:, j : j + 1]

    def one_block(block):
        queries = query_ref[pl.ds(block * BLOCK, BLOCK)].astype(jnp.float32)
        heads = [
            queries[:, j * GROUP : (j + 1) * GROUP].reshape(BLOCK_ROWS, HEAD_DIM)
            for j in range(KV_HEADS)
        ]
        scores = [
            jnp.dot(
                side_by_side(heads[2 * i], heads[2 * i + 1]),
                key_ref[i * PAIR_DIM : (i + 1) * PAIR_DIM],
                preferred_element_type=jnp.float32,
            )
            for i in range(PAIRS)
        ]
        peaks, totals = [], []
        for i in range(PAIRS):
            peak = jnp.max(scores[i], axis=1, keepdims=True)
            expo = jnp.exp((scores[i] - peak) * SCALE)
            total = jnp.sum(expo, axis=1, keepdims=True)
            output = jnp.dot(
                expo.astype(jnp.bfloat16),
                value_ref[:, i * PAIR_DIM : (i + 1) * PAIR_DIM],
                preferred_element_type=jnp.float32,
            )
            for r in range(BLOCK):
                for h in range(2):
                    rows = slice(h * BLOCK_ROWS + r * GROUP, h * BLOCK_ROWS + (r + 1) * GROUP)
                    chunk = ((block * BLOCK + r) * KV_HEADS + 2 * i + h) * ROWS
                    out_ref[pl.ds(chunk, GROUP)] = output[rows, columns(h)] * shrink
            peaks += [peak[:BLOCK_ROWS], peak[BLOCK_ROWS:]]
            totals += [total[:BLOCK_ROWS], total[BLOCK_ROWS:]]
        sums_ref[:BLOCK_ROWS] = in_lanes(peaks, BLOCK_ROWS)
        sums_ref[BLOCK_ROWS:] = in_lanes(totals, BLOCK_ROWS)
        sums = sums_ref[...].T[:GROUP]
        if count == BLOCK:
            join_own()
        else:
            pl.when(me // BLOCK == block)(join_own)
        here = me // BLOCK == block
        own_peaks = jnp.where(here, own_flat_ref[1], LOWEST)
        own_totals = jnp.where(here, own_flat_ref[0], 0.0)
        peaks = both_halves(sums)
        joined = jnp.maximum(peaks, own_peaks)
        totals = sums * jnp.exp((peaks - joined) * SCALE)
        totals += own_totals * jnp.exp((own_peaks - joined) * SCALE)
        lane = lax.broadcasted_iota(jnp.int32, (GROUP, HEAD_DIM), 1)
        weights = joined + jnp.where(
            lane < BLOCK_ROWS, own_sums_ref[2], jnp.log(totals) * (1.0 / SCALE)
        )
        coarse = jnp.round(weights * (1.0 / COARSE)) * COARSE
        fine = weights - coarse
        for r in range(BLOCK):
            for j in range(KV_HEADS):
                chunk = ((block * BLOCK + r) * KV_HEADS + j) * ROWS
                out_ref[pl.ds(chunk + GROUP, 1)] = coarse[j : j + 1]
                out_ref[pl.ds(chunk + GROUP + 1, 1)] = fine[j : j + 1]

    if count == BLOCK:
        one_block(0)
    else:
        pl.loop(0, count // BLOCK)(one_block)


def join_kernel(parts_ref, out_ref):
    parts = parts_ref.shape[0] // ROWS

    def every(row):
        return parts_ref[pl.ds(row, parts, stride=ROWS)]

    weights = every(GROUP) + every(GROUP + 1)
    totals = pltpu.roll(weights, HEAD_DIM - BLOCK_ROWS, 1)
    top = jnp.max(totals, axis=0, keepdims=True)
    total = jnp.sum(jnp.exp((totals - top) * SCALE), axis=0, keepdims=True)
    factor = jnp.exp((weights - top) * SCALE) / total
    first = (lax.axis_index("seq") % BLOCK) * GROUP
    for h in range(GROUP):
        lane = jnp.full(factor.shape, first + h, jnp.int32)
        output = every(h) * jnp.take_along_axis(factor, lane, axis=1)
        output = jnp.sum(output, axis=0, keepdims=True)
        out_ref[:, h * HEAD_DIM : (h + 1) * HEAD_DIM] = output.astype(out_ref.dtype)


def straight(seq, grp, even, odd):
    return [
        (i * grp + j, (i ^ (odd if j % 2 else even)) * grp + j) for i in range(seq) for j in range(grp)
    ]


def on_device(seq, grp, queries, prompt_keys, prompt_values, suffix_keys, suffix_values, lengths):
    span = suffix_keys.shape[1]
    width = KV_HEADS * HEAD_DIM
    rows, length, own_keys, own_values, keys, values = pl.pallas_call(
        load_kernel,
        compiler_params=LIMIT,
        out_shape=(
            pltpu.VMEM((1, Q_HEADS, HEAD_DIM), queries.dtype),
            pltpu.VMEM((GROUP, HEAD_DIM), jnp.int32),
            pltpu.VMEM((span, width), suffix_keys.dtype),
            pltpu.VMEM((span, width), suffix_values.dtype),
            pltpu.VMEM(prompt_keys.shape[::-1], prompt_keys.dtype),
            pltpu.VMEM(prompt_values.shape, prompt_values.dtype),
        ),
        in_specs=[HBM, ANY] + [HBM] * 4,
        out_specs=(VMEM,) * 6,
        scratch_shapes=[
            pltpu.VMEM(queries.shape, queries.dtype),
            pltpu.VMEM((1, 1), jnp.int32),
            pltpu.VMEM(prompt_keys.shape, prompt_keys.dtype),
            pltpu.SemaphoreType.DMA((6,)),
        ],
    )(
        in_hbm(queries),
        lengths.reshape(1, 1),
        in_hbm(suffix_keys.reshape(span, width)),
        in_hbm(suffix_values.reshape(span, width)),
        in_hbm(prompt_keys),
        in_hbm(prompt_values),
    )
    scratch = [pltpu.VMEM((2 * BLOCK_ROWS, HEAD_DIM), jnp.float32)]
    if seq == BLOCK and grp % 2 == 0:
        direct = [
            lax.ppermute(queries, ("seq", "grp"), straight(seq, grp, even, odd)) for even, odd in DIRECT
        ]
        shared = lax.ppermute(queries, ("seq", "grp"), straight(seq, grp, SHARED, SHARED))
        near, mine = pl.pallas_call(
            collect_kernel,
            compiler_params=LIMIT,
            out_shape=(
                pltpu.VMEM((2, Q_HEADS, HEAD_DIM), queries.dtype),
                pltpu.VMEM((len(DIRECT), Q_HEADS, HEAD_DIM), queries.dtype),
            ),
            in_specs=[VMEM] * (2 + len(DIRECT)),
            out_specs=(VMEM, VMEM),
        )(in_vmem(rows), *[in_vmem([*direct, shared][i]) for i in ORDER])
        other = lax.ppermute(mine, "grp", [(j, j ^ 1) for j in range(grp)])
        own_rows, every = near, [near, mine, other]
        scratch.append(pltpu.VMEM((seq, Q_HEADS, HEAD_DIM), queries.dtype))
    else:
        copies = pl.pallas_call(
            spread_kernel,
            compiler_params=LIMIT,
            out_shape=pltpu.VMEM((seq, Q_HEADS, HEAD_DIM), queries.dtype),
            in_specs=[VMEM],
            out_specs=VMEM,
        )(queries)
        own_rows, every = rows, [lax.all_to_all(copies, "seq", 0, 0, tiled=True)]
    own, own_sums, own_flat = pl.pallas_call(
        own_kernel,
        compiler_params=LIMIT,
        out_shape=(
            pltpu.VMEM((KV_HEADS, GROUP, HEAD_DIM), jnp.float32),
            pltpu.VMEM((4, GROUP, HEAD_DIM), jnp.float32),
            pltpu.VMEM((2, GROUP, HEAD_DIM), jnp.float32),
        ),
        in_specs=[VMEM] * 5,
        out_specs=(VMEM,) * 3,
        scratch_shapes=[pltpu.VMEM((2 * BLOCK_ROWS, HEAD_DIM), jnp.float32)],
    )(*map(in_vmem, (length, own_rows, own_keys, own_values, values)))
    partial = pl.pallas_call(
        functools.partial(partial_kernel, len(every) == 1),
        compiler_params=LIMIT,
        out_shape=pltpu.VMEM((seq * grp * ROWS, HEAD_DIM), jnp.float32),
        in_specs=[VMEM] * (5 + len(every)),
        out_specs=VMEM,
        scratch_shapes=scratch,
    )(in_vmem(keys), in_vmem(values), *map(in_vmem, (own, own_sums, own_flat, *every)))
    partial = partial.reshape(seq * grp, ROWS // 2, 2, HEAD_DIM).astype(jnp.float16)
    parts = lax.all_to_all(partial, ("seq", "grp"), 0, 0, tiled=True)
    parts = parts.astype(jnp.float32).reshape(seq * grp * ROWS, HEAD_DIM)
    return pl.pallas_call(
        join_kernel,
        compiler_params=LIMIT,
        out_shape=jax.ShapeDtypeStruct((1, GROUP * HEAD_DIM), queries.dtype),
        in_specs=[VMEM],
        out_specs=VMEM,
    )(in_vmem(parts))


def solution(mesh):
    in_specs = (
        P("seq", None),
        P(("seq", "grp"), None),
        P(("seq", "grp"), None),
        P("seq", "grp", None),
        P("seq", "grp", None),
        P("seq"),
    )
    return jax.shard_map(
        functools.partial(on_device, mesh.shape["seq"], mesh.shape["grp"]),
        mesh=mesh,
        in_specs=in_specs,
        out_specs=P("seq", "grp"),
        check_vma=False,
    )
```
